256 devices in a mesh: prow: 8 (over x, core), pcol: 32 (over y, z).
Axes of the slice: x: 4, y: 4, z: 8, core: 2. Of those that a mesh axis runs over, the one named last changes fastest.
Arguments:
- leaf_rhs: float32 [8192, 1024], P('prow'), may hold values from -6 to 6
- leaf_inverse: float32 [8192, 256], P(('prow', 'pcol')), may hold values from -0.375 to 0.375
- parent_rhs: float32 [32, 2048, 1024], P('pcol', 'prow'), may hold values from -6 to 6
- parent_inverse: float32 [32, 2048, 256], P('pcol', 'prow'), may hold values from -0.375 to 0.375
- factor: float32 [32, 2048, 8192], P('pcol', None, 'prow'), may hold values from -0.0234375 to 0.0234375
- tile_mask: int32 [32, 8, 32], P('pcol', None, 'prow'), may hold values from 0 to 1, as said below
Outputs:
- parent_solution: float32 [32, 2048, 1024], P('pcol', 'prow')
- leaf_solution: float32 [8192, 1024], P(('prow', 'pcol'))
The draws below stay inside these ranges and needn't reach their ends.
Inputs may be any that keep to these rules, and one draw needn't show every extreme that they name: `tile_mask`: 1 marks a stored factor tile, 0 an absent one.
All inputs are finite; a program needn't handle non-finite values.
Results may differ from the reference program's by a relative error of at most 0.0001.
Values sent between devices are 32-bit elements; how exact they have to be, the bound alone decides.
A program may use at most 192 MiB of HBM per device.

```python
import jax
import jax.numpy as jnp
from jax import lax

BS = 256
RHS = 1024
GR = 8
GC = 32
NL = 32
NP = 256


def draw_tile_mask(key, part):
    key = jax.random.fold_in(key, 11)
    level_key, entry_key = jax.random.split(key)
    levels = jax.random.randint(level_key, (GC, 1, 1), 1, 4)
    entries = jax.random.randint(entry_key, (GC, GR, NL), 0, 4)
    return (entries < levels).astype(jnp.int32)


def shard_levels(key, shape, cuts, least, top_value):
    level, own = 1.0, jax.random.fold_in(key, 6)
    for axis_at, blocks in cuts:
        heights = jnp.exp(jax.random.uniform(jax.random.fold_in(own, axis_at), (blocks,), jnp.float32, least / len(cuts), top_value / len(cuts)))
        level = level * jnp.repeat(heights, shape[axis_at] // blocks).reshape([-1 if axis == axis_at else 1 for axis in range(len(shape))])
    return level


def bell_draw(stream_key, extent, spread, bound, cuts=(), dtype=jnp.bfloat16):
    result = jax.random.normal(stream_key, extent, jnp.float32) * spread
    if len(cuts) > 0:
        result = shard_levels(stream_key, extent, cuts, -0.22, 0.18) * result
    return jnp.clip(result, min=-bound, max=bound).astype(dtype)


def setup_inputs(seed: int = 0) -> dict:
    key_list = jax.random.split(jax.random.key(seed), 7)
    leaf_rhs = bell_draw(key_list[0], (NL * BS, RHS), 1.0, 6.0, ((0, 8),), jnp.float32)
    leaf_inverse = bell_draw(key_list[1], (NL * BS, BS), BS ** -0.5, 0.375, ((0, 256),), jnp.float32)
    parent_rhs = bell_draw(key_list[2], (GC, GR * BS, RHS), 1.0, 6.0, ((0, 32), (1, 8)), jnp.float32)
    parent_inverse = bell_draw(key_list[3], (GC, GR * BS, BS), BS ** -0.5, 0.375, ((0, 32), (1, 8)), jnp.float32)
    factor = bell_draw(key_list[4], (GC, GR * BS, NL * BS), (BS * (NL + NP)) ** -0.5, 0.0234375, ((0, 32), (2, 8)), jnp.float32)
    tile_mask = draw_tile_mask(jax.random.fold_in(key_list[6], 71), 0)
    return dict(leaf_rhs=leaf_rhs, leaf_inverse=leaf_inverse, parent_rhs=parent_rhs, parent_inverse=parent_inverse, factor=factor, tile_mask=tile_mask)


def reference(leaf_rhs, leaf_inverse, parent_rhs, parent_inverse, factor, tile_mask):
    highest = lax.Precision.HIGHEST
    leaf_inv = leaf_inverse.reshape(NL, BS, BS)
    leaf_forward = jnp.einsum('iab,ibn->ian', leaf_inv, leaf_rhs.reshape(NL, BS, RHS), precision=highest)
    mask_values = tile_mask.astype(jnp.float32)

    def column_update(operands):
        tiles, masks = operands
        tile_four = tiles.reshape(GR, BS, NL, BS)
        products = jnp.einsum('raib,ibn->rain', tile_four, leaf_forward, precision=highest)
        return jnp.einsum('rain,ri->ran', products, masks, precision=highest)

    update = lax.map(column_update, (factor, mask_values))
    residue = parent_rhs.reshape(GC, GR, BS, RHS) - update
    parent_inv = parent_inverse.reshape(GC, GR, BS, BS)
    parent_forward = jnp.einsum('crab,crbn->cran', parent_inv, residue, precision=highest)
    parent_back = jnp.einsum('crba,crbn->cran', parent_inv, parent_forward, precision=highest)

    def column_back(running, operands):
        tiles, masks, solved = operands
        tile_four = tiles.reshape(GR, BS, NL, BS)
        weighted = jnp.einsum('ran,ri->rian', solved, masks, precision=highest)
        return running + jnp.einsum('raib,rian->ibn', tile_four, weighted, precision=highest), None

    zeroes = jnp.zeros((NL, BS, RHS), jnp.float32)
    leaf_update, unused = lax.scan(column_back, zeroes, (factor, mask_values, parent_back))
    remaining = leaf_forward - leaf_update
    leaf_back = jnp.einsum('iba,ibn->ian', leaf_inv, remaining, precision=highest)
    return parent_back.reshape(GC, GR * BS, RHS), leaf_back.reshape(NL * BS, RHS)
```

```python
import jax
import jax.numpy as jnp
from jax import lax
from jax.experimental import pallas as pl
from jax.experimental.pallas import tpu as pltpu
from jax.sharding import PartitionSpec as P

MESH = pl.DeviceIdType.MESH
F32 = jnp.float32
BF16 = jnp.bfloat16
BS = 256
W = 128
N = 8
HB = BS // 2
ROWS = 32

(PAIR, XA, XB, MB, MA, PA, PB, GP, GM, GC, HA, HBK, FM, FP, FO, YXA, YXB, YMB, YMA, YPA, YPB, Z1) = range(22)
KINDS = Z1 + 7


def split(v):
    hi = v.astype(BF16)
    return hi, (v - hi.astype(F32)).astype(BF16)


def dot(a, b):
    return jnp.dot(a, b, preferred_element_type=F32)


def pair_of(v):
    return jnp.concatenate(split(v), axis=1)


def dot2(a, b):
    r = dot(a, b)
    return r[:, :W] + r[:, W:]


def dot1(a, b):
    return dot2(a, jnp.concatenate([b, b], axis=0))


ORDER = (
    ("forward", 0), ("opposite", 6), ("relay", 5), ("stage1", 0), ("z_send", 10),
    ("y_stage2", 8), ("solve", 3), ("finish", 13), ("stage2", 1), ("backward", 6),
)


def kernel(
    mask_in, rhs, inv, prhs, pinv, fac, out_p, out_l,
    f2, ft2, s_all, t_all, u_all, pair, xa, xb, ym, yp, yxa, yxb, yym, yyp, zr,
    inv_all, i2, it2, l2, s2, res, p2, pt2, d_all, mask,
    load_sem, out_sem, a_send, a_recv, send, recv,
):
    p = lax.axis_index("prow")
    q = lax.axis_index("pcol")
    x, k = p // 2, lax.rem(p, 2)
    y, z = q // 8, lax.rem(q, 8)
    xp, xm, xo = lax.rem(x + 1, 4), lax.rem(x + 3, 4), lax.rem(x + 2, 4)
    yp_i, ym_i, yo = lax.rem(y + 1, 4), lax.rem(y + 3, 4), lax.rem(y + 2, 4)
    dev_c = (x * 2 + 1 - k, q)
    dev_xp, dev_xm = (xp * 2 + k, q), (xm * 2 + k, q)
    dev_yp, dev_ym = (p, yp_i * 8 + z), (p, ym_i * 8 + z)

    def z_at(j):
        return lax.rem(z + j, 8)

    def dev_z(j):
        return (p, y * 8 + z_at(j))

    def dev_y(j):
        return (p, lax.rem(y + j, 4) * 8 + z)

    lo, up = pl.ds(0, HB), pl.ds(HB, HB)
    own = k * 4

    def rows(at, start=0, size=BS):
        return pl.ds(pl.multiple_of(at * BS + start, HB), size)

    def copy(kind, t):
        def go(src, dst, dev):
            return pltpu.make_async_remote_copy(
                src_ref=src, dst_ref=dst, send_sem=send.at[t, kind], recv_sem=recv.at[t, kind],
                device_id=dev, device_id_type=MESH,
            )

        if kind == PAIR:
            return go(u_all.at[t, 1 - k], pair.at[t], dev_c)
        if kind == XA:
            return go(u_all.at[t, k, rows(xo, 0, HB)], xa.at[t], dev_xp)
        if kind == XB:
            return go(u_all.at[t, k, rows(xo, HB, HB)], xb.at[t], dev_xm)
        if kind == MB:
            return go(u_all.at[t, k, rows(xp, HB, HB)], ym.at[t, up], dev_xp)
        if kind == MA:
            return go(u_all.at[t, k, rows(xp, 0, HB)], ym.at[t, lo], dev_xp)
        if kind == PA:
            return go(u_all.at[t, k, rows(xm, 0, HB)], yp.at[t, lo], dev_xm)
        if kind == PB:
            return go(u_all.at[t, k, rows(xm, HB, HB)], yp.at[t, up], dev_xm)
        if kind in (GP, GM, GC):
            ref = s_all.at[t, own + x]
            return go(ref, ref, {GP: dev_xp, GM: dev_xm, GC: dev_c}[kind])
        if kind == HA:
            ref = s_all.at[t, own + xm, lo]
            return go(ref, ref, dev_xp)
        if kind == HBK:
            ref = s_all.at[t, own + xp, up]
            return go(ref, ref, dev_xm)
        if kind in (FM, FP, FO):
            ref = s_all.at[t, own + {FM: xm, FP: xp, FO: xo}[kind]]
            return go(ref, ref, dev_c)
        if kind == YXA:
            return go(t_all.at[t, yo, lo], yxa.at[t], dev_yp)
        if kind == YXB:
            return go(t_all.at[t, yo, up], yxb.at[t], dev_ym)
        if kind == YMB:
            return go(t_all.at[t, yp_i, up], yym.at[t, up], dev_yp)
        if kind == YMA:
            return go(t_all.at[t, yp_i, lo], yym.at[t, lo], dev_yp)
        if kind == YPA:
            return go(t_all.at[t, ym_i, lo], yyp.at[t, lo], dev_ym)
        if kind == YPB:
            return go(t_all.at[t, ym_i, up], yyp.at[t, up], dev_ym)
        j = kind - Z1 + 1
        return go(t_all.at[t, y, pl.ds(z_at(j) * ROWS, ROWS)], zr.at[t, j - 1], dev_z(j))

    def start(t, *kinds):
        for kind in kinds:
            copy(kind, t).start()

    def arrived(t, *kinds):
        for kind in kinds:
            copy(kind, t).wait_recv()

    def load_f(i):
        return pltpu.make_async_copy(
            fac.at[:, :, pl.ds(i * W, W)], s_all.at[i], load_sem.at[i]
        )

    def load_r(t):
        return pltpu.make_async_copy(
            rhs.at[:, :, pl.ds(t * W, W)], t_all.at[t], load_sem.at[N + t]
        )

    def load_p(t):
        return pltpu.make_async_copy(
            prhs.at[:, pl.ds(t * W, W)], res.at[t], load_sem.at[2 * N + t]
        )

    load_m = pltpu.make_async_copy(mask_in, mask, load_sem.at[3 * N])
    load_m.start()
    for i in range(N):
        load_f(i).start()
    for t in range(N):
        load_r(t).start()
    for t in range(N):
        load_p(t).start()

    barrier = pltpu.get_barrier_semaphore()
    others = [dev_c, dev_xp, dev_xm]
    others += [dev_y(j) for j in range(1, 4)] + [dev_z(j) for j in range(1, 8)]
    for dev in others:
        pl.semaphore_signal(barrier, inc=1, device_id=dev, device_id_type=MESH)
    mine = pl.ds(pl.multiple_of(z * ROWS, ROWS), ROWS)
    inv_all[y, mine, :] = inv[...]
    pl.semaphore_wait(barrier, len(others))

    def piece(j, way):
        at = pl.ds(pl.multiple_of(lax.rem(z + 8 - j, 8) * ROWS, ROWS), ROWS)
        ref = inv_all.at[y, at]
        return pltpu.make_async_remote_copy(
            src_ref=ref, dst_ref=ref, send_sem=a_send.at[j, way], recv_sem=a_recv.at[j, way],
            device_id=dev_y(way) if way else dev_z(j), device_id_type=MESH,
        )

    def over_y(j):
        for way in (1, 3, 2):
            piece(j, way).start()

    def over_z(j):
        return pltpu.make_async_remote_copy(
            src_ref=inv_all.at[y, mine], dst_ref=inv_all.at[y, mine],
            send_sem=a_send.at[j, 0], recv_sem=a_recv.at[j, 0],
            device_id=dev_z(j), device_id_type=MESH,
        )

    for j in (1, 7, 2, 6, 3, 5, 4):
        over_z(j).start()
    over_y(0)

    def tiles(i):
        load_f(2 * i).wait()
        load_f(2 * i + 1).wait()

        @pl.loop(0, 8)
        def _(s):
            r = lax.rem(s, 4) * 2 + s // 4
            v = jnp.concatenate([s_all[2 * i, r], s_all[2 * i + 1, r]], axis=1)
            v = v * mask[0, r, i].astype(F32)
            here = rows(lax.rem(s, 4))
            hi, low = split(v)
            f2[s // 4, here, i * BS : (i + 1) * BS] = hi
            f2[s // 4, here, (4 + i) * BS : (5 + i) * BS] = low
            hi, low = split(v.T)
            half = slice(i % 2 * BS, (i % 2 + 1) * BS)
            ft2[i // 2, half, rows(s)] = hi
            ft2[i // 2, half, rows(8 + s)] = low

    load_m.wait()
    tiles(0)
    for j in (1, 7):
        over_z(j).wait_recv()
        over_y(j)
    tiles(1)
    for j in (2, 6, 3, 5):
        over_z(j).wait_recv()
        over_y(j)
    v = pinv[...]
    p2[...] = pair_of(v)
    pt2[...] = pair_of(v.T)
    over_z(4).wait_recv()
    over_y(4)
    tiles(2)
    tiles(3)
    for t in range(N):
        load_r(t).wait()
        load_p(t).wait()
    for j in range(8):
        for way in (1, 2, 3):
            piece(j, way).wait_recv()

    @pl.loop(0, 4)
    def _(i):
        v = inv_all[i]
        i2[i] = pair_of(v)
        it2[i] = pair_of(v.T)

    def forward(t):
        @pl.loop(0, 4)
        def _(i):
            b = pair_of(dot1(i2[i], pair_of(t_all[t, i])))
            l2[rows(i), :] = b
            l2[rows(4 + i), :] = b

        d_all[t] = dot1(it2[y, mine], l2[rows(y), :])
        u_all[t, 1 - k] = dot2(f2[1 - k], l2[...])
        start(t, PAIR)
        u_all[t, k] = dot2(f2[k], l2[...])

    def add(ref, at, other):
        ref[at] = ref[at] + other

    def stage1(t):
        arrived(t, PAIR)
        u, got = u_all.at[t, k], pair.at[t]
        add(u, rows(xo), got[rows(xo)])
        start(t, XA, XB)
        add(u, rows(xp), got[rows(xp)])
        add(u, rows(xm), got[rows(xm)])
        start(t, MB, PA)
        add(u, rows(x), got[rows(x)])

    def stage2(t):
        arrived(t, XA)
        add(u_all.at[t, k], rows(xp, 0, HB), xa[t])
        start(t, MA)
        arrived(t, XB)
        add(u_all.at[t, k], rows(xm, HB, HB), xb[t])
        start(t, PB)

    def keep(t):
        return pltpu.make_async_copy(s_all.at[t, own + x], out_p.at[:, pl.ds(t * W, W)], out_sem.at[t])

    def solve(t):
        arrived(t, MA, MB, PA, PB)
        v = res[t] - ((u_all[t, k, rows(x)] + ym[t]) + yp[t])
        v = dot1(p2[...], pair_of(v))
        s_all[t, own + x] = dot1(pt2[...], pair_of(v))
        start(t, GP, GM, GC)
        keep(t).start()

    def relay(t):
        arrived(t, GP)
        start(t, HA, FM)
        arrived(t, GM)
        start(t, HBK, FP)

    def opposite(t):
        arrived(t, HA, HBK)
        start(t, FO)

    def backward(t):
        arrived(t, GC, FM, FP, FO)

        @pl.loop(0, 8)
        def _(s):
            b = pair_of(s_all[t, s])
            s2[rows(s), :] = b
            s2[rows(8 + s), :] = b

        @pl.loop(0, 2)
        def _(i):
            v = dot2(ft2[i], s2[...])
            t_all[t, 2 * i] = dot1(it2[2 * i], pair_of(v[:BS]))
            t_all[t, 2 * i + 1] = dot1(it2[2 * i + 1], pair_of(v[BS:]))

        start(t, YXA, YXB, YMB, YPA)

    def y_stage2(t):
        arrived(t, YXA)
        t_all[t, yp_i, lo] = t_all[t, yp_i, lo] + yxa[t]
        start(t, YMA)
        arrived(t, YXB)
        t_all[t, ym_i, up] = t_all[t, ym_i, up] + yxb[t]
        start(t, YPB)

    def z_send(t):
        arrived(t, YMA, YMB, YPA, YPB)
        t_all[t, y] = (t_all[t, y] + yym[t]) + yyp[t]
        start(t, *range(Z1, Z1 + 7))

    def finish(t):
        arrived(t, *range(Z1, Z1 + 7))
        total = t_all[t, y, mine]
        for j in range(7):
            total = total + zr[t, j]
        out_l[:, pl.ds(pl.multiple_of(t * W, W), W)] = d_all[t] - total

    stages = dict(
        forward=forward, stage1=stage1, stage2=stage2, solve=solve, relay=relay, opposite=opposite,
        backward=backward, y_stage2=y_stage2, z_send=z_send, finish=finish,
    )

    @pl.loop(0, N + max(lag for _, lag in ORDER))
    def _(step):
        for name, lag in ORDER:
            t = step - lag

            @pl.when(jnp.logical_and(t >= 0, t < N))
            def _():
                stages[name](t)

    for j in range(8):
        for way in range(4):
            if j or way:
                (piece(j, way) if way else over_z(j)).wait_send()

    @pl.loop(0, N)
    def _(t):
        keep(t).wait()
        for kind in range(KINDS):
            copy(kind, t).wait_send()


def body(leaf_rhs, leaf_inverse, parent_rhs, parent_inverse, factor, tile_mask):
    vmem = pl.BlockSpec(memory_space=pltpu.VMEM)
    hbm = pl.BlockSpec(memory_space=pl.ANY)
    f32, b16 = (lambda *s: pltpu.VMEM(s, F32)), (lambda *s: pltpu.VMEM(s, BF16))
    dma = lambda *s: pltpu.SemaphoreType.DMA(s)
    solved, leaf = pl.pallas_call(
        kernel,
        out_shape=(
            jax.ShapeDtypeStruct((BS, N * W), F32),
            jax.ShapeDtypeStruct((ROWS, N * W), F32),
        ),
        in_specs=[hbm, hbm, vmem, hbm, vmem, hbm],
        out_specs=(hbm, vmem),
        scratch_shapes=[
            b16(2, 4 * BS, 8 * BS),
            b16(2, 2 * BS, 16 * BS),
            f32(N, 8, BS, W),
            f32(N, 4, BS, W),
            f32(N, 2, 4 * BS, W),
            f32(N, 4 * BS, W),
            f32(N, HB, W), f32(N, HB, W),
            f32(N, BS, W), f32(N, BS, W),
            f32(N, HB, W), f32(N, HB, W),
            f32(N, BS, W), f32(N, BS, W),
            f32(N, 7, ROWS, W),
            f32(4, BS, BS),
            b16(4, BS, 2 * BS), b16(4, BS, 2 * BS),
            b16(8 * BS, 2 * W),
            b16(16 * BS, 2 * W),
            f32(N, BS, W),
            b16(BS, 2 * BS), b16(BS, 2 * BS),
            f32(N, ROWS, W),
            pltpu.SMEM((1, 8, 4), jnp.int32),
            dma(3 * N + 1), dma(N), dma(8, 4), dma(8, 4), dma(N, KINDS), dma(N, KINDS),
        ],
        compiler_params=pltpu.CompilerParams(
            collective_id=0, has_side_effects=True, vmem_limit_bytes=63 * 2**20
        ),
    )(
        tile_mask,
        leaf_rhs.reshape(4, BS, N * W),
        leaf_inverse,
        parent_rhs[0],
        parent_inverse[0],
        factor[0].reshape(8, BS, 4 * BS),
    )
    return solved[None], leaf


def solution(mesh):
    placed = (
        P("prow", None),
        P(("prow", "pcol"), None),
        P("pcol", "prow", None),
        P("pcol", "prow", None),
        P("pcol", None, "prow"),
        P("pcol", None, "prow"),
    )
    return jax.shard_map(
        body,
        mesh=mesh,
        in_specs=placed,
        out_specs=(P("pcol", "prow", None), P(("prow", "pcol"), None)),
        check_vma=False,
    )
```

```python
import jax
import jax.numpy as jnp
from jax import lax
from jax.experimental import pallas as pl
from jax.experimental.pallas import tpu as pltpu
from jax.sharding import PartitionSpec as P

MESH = pl.DeviceIdType.MESH
F32 = jnp.float32
BF16 = jnp.bfloat16
BS = 256
W = 128
N = 8
HB = BS // 2
ROWS = 32

(PAIR, XA, XB, MB, MA, PA, PB, GP, GM, GC, HA, HBK, FM, FP, FO, YXA, YXB, YMB, YMA, YPA, YPB, Z1) = range(22)
KINDS = Z1 + 7


def split(v):
    hi = v.astype(BF16)
    return hi, (v - hi.astype(F32)).astype(BF16)


def dot(a, b):
    return jnp.dot(a, b, preferred_element_type=F32)


def pair_of(v):
    return jnp.concatenate(split(v), axis=1)


def dot2(a, b):
    r = dot(a, b)
    return r[:, :W] + r[:, W:]


def dot1(a, b):
    return dot2(a, jnp.concatenate([b, b], axis=0))


ORDER = (
    ("forward", 0), ("opposite", 6), ("relay", 5), ("stage1", 0), ("z_send", 10),
    ("y_stage2", 8), ("solve", 3), ("finish", 13), ("stage2", 1), ("backward", 6),
)


def kernel(
    mask_in, rhs, inv, prhs, pinv, fac, out_p, out_l,
    f2, ft2, s_all, t_all, u_all, pair, xa, xb, ym, yp, yxa, yxb, yym, yyp, zr,
    inv_all, i2, it2, l2, s2, res, p2, pt2, d_all, mask,
    load_sem, out_sem, a_send, a_recv, send, recv,
):
    p = lax.axis_index("prow")
    q = lax.axis_index("pcol")
    x, k = p // 2, lax.rem(p, 2)
    y, z = q // 8, lax.rem(q, 8)
    xp, xm, xo = lax.rem(x + 1, 4), lax.rem(x + 3, 4), lax.rem(x + 2, 4)
    yp_i, ym_i, yo = lax.rem(y + 1, 4), lax.rem(y + 3, 4), lax.rem(y + 2, 4)
    dev_c = (x * 2 + 1 - k, q)
    dev_xp, dev_xm = (xp * 2 + k, q), (xm * 2 + k, q)
    dev_yp, dev_ym = (p, yp_i * 8 + z), (p, ym_i * 8 + z)

    def z_at(j):
        return lax.rem(z + j, 8)

    def dev_z(j):
        return (p, y * 8 + z_at(j))

    def dev_y(j):
        return (p, lax.rem(y + j, 4) * 8 + z)

    lo, up = pl.ds(0, HB), pl.ds(HB, HB)
    own = k * 4

    def rows(at, start=0, size=BS):
        return pl.ds(pl.multiple_of(at * BS + start, HB), size)

    def copy(kind, t):
        def go(src, dst, dev):
            return pltpu.make_async_remote_copy(
                src_ref=src, dst_ref=dst, send_sem=send.at[t, kind], recv_sem=recv.at[t, kind],
                device_id=dev, device_id_type=MESH,
            )

        if kind == PAIR:
            return go(u_all.at[t, 1 - k], pair.at[t], dev_c)
        if kind == XA:
            return go(u_all.at[t, k, rows(xo, 0, HB)], xa.at[t], dev_xp)
        if kind == XB:
            return go(u_all.at[t, k, rows(xo, HB, HB)], xb.at[t], dev_xm)
        if kind == MB:
            return go(u_all.at[t, k, rows(xp, HB, HB)], ym.at[t, up], dev_xp)
        if kind == MA:
            return go(u_all.at[t, k, rows(xp, 0, HB)], ym.at[t, lo], dev_xp)
        if kind == PA:
            return go(u_all.at[t, k, rows(xm, 0, HB)], yp.at[t, lo], dev_xm)
        if kind == PB:
            return go(u_all.at[t, k, rows(xm, HB, HB)], yp.at[t, up], dev_xm)
        if kind in (GP, GM, GC):
            ref = s_all.at[t, own + x]
            return go(ref, ref, {GP: dev_xp, GM: dev_xm, GC: dev_c}[kind])
        if kind == HA:
            ref = s_all.at[t, own + xm, lo]
            return go(ref, ref, dev_xp)
        if kind == HBK:
            ref = s_all.at[t, own + xp, up]
            return go(ref, ref, dev_xm)
        if kind in (FM, FP, FO):
            ref = s_all.at[t, own + {FM: xm, FP: xp, FO: xo}[kind]]
            return go(ref, ref, dev_c)
        if kind == YXA:
            return go(t_all.at[t, yo, lo], yxa.at[t], dev_yp)
        if kind == YXB:
            return go(t_all.at[t, yo, up], yxb.at[t], dev_ym)
        if kind == YMB:
            return go(t_all.at[t, yp_i, up], yym.at[t, up], dev_yp)
        if kind == YMA:
            return go(t_all.at[t, yp_i, lo], yym.at[t, lo], dev_yp)
        if kind == YPA:
            return go(t_all.at[t, ym_i, lo], yyp.at[t, lo], dev_ym)
        if kind == YPB:
            return go(t_all.at[t, ym_i, up], yyp.at[t, up], dev_ym)
        j = kind - Z1 + 1
        return go(t_all.at[t, y, pl.ds(z_at(j) * ROWS, ROWS)], zr.at[t, j - 1], dev_z(j))

    def start(t, *kinds):
        for kind in kinds:
            copy(kind, t).start()

    def arrived(t, *kinds):
        for kind in kinds:
            copy(kind, t).wait_recv()

    def load_f(i):
        return pltpu.make_async_copy(
            fac.at[:, :, pl.ds(i * W, W)], s_all.at[i], load_sem.at[i]
        )

    def load_r(t):
        return pltpu.make_async_copy(
            rhs.at[:, :, pl.ds(t * W, W)], t_all.at[t], load_sem.at[N + t]
        )

    def load_p(t):
        return pltpu.make_async_copy(
            prhs.at[:, pl.ds(t * W, W)], res.at[t], load_sem.at[2 * N + t]
        )

    load_m = pltpu.make_async_copy(mask_in, mask, load_sem.at[3 * N])
    load_m.start()
    for i in range(N):
        load_f(i).start()
    for t in range(N):
        load_r(t).start()
    for t in range(N):
        load_p(t).start()

    barrier = pltpu.get_barrier_semaphore()
    others = [dev_c, dev_xp, dev_xm]
    others += [dev_y(j) for j in range(1, 4)] + [dev_z(j) for j in range(1, 8)]
    for dev in others:
        pl.semaphore_signal(barrier, inc=1, device_id=dev, device_id_type=MESH)
    mine = pl.ds(pl.multiple_of(z * ROWS, ROWS), ROWS)
    inv_all[y, mine, :] = inv[...]
    pl.semaphore_wait(barrier, len(others))

    def piece(j, way):
        at = pl.ds(pl.multiple_of(lax.rem(z + 8 - j, 8) * ROWS, ROWS), ROWS)
        ref = inv_all.at[y, at]
        return pltpu.make_async_remote_copy(
            src_ref=ref, dst_ref=ref, send_sem=a_send.at[j, way], recv_sem=a_recv.at[j, way],
            device_id=dev_y(way) if way else dev_z(j), device_id_type=MESH,
        )

    def over_y(j):
        for way in (1, 3, 2):
            piece(j, way).start()

    def over_z(j):
        return pltpu.make_async_remote_copy(
            src_ref=inv_all.at[y, mine], dst_ref=inv_all.at[y, mine],
            send_sem=a_send.at[j, 0], recv_sem=a_recv.at[j, 0],
            device_id=dev_z(j), device_id_type=MESH,
        )

    for j in (1, 7, 2, 6, 3, 5, 4):
        over_z(j).start()
    over_y(0)

    def tiles(i):
        load_f(2 * i).wait()
        load_f(2 * i + 1).wait()

        @pl.loop(0, 8)
        def _(s):
            r = lax.rem(s, 4) * 2 + s // 4
            v = jnp.concatenate([s_all[2 * i, r], s_all[2 * i + 1, r]], axis=1)
            v = v * mask[0, i, r].astype(F32)
            here = rows(lax.rem(s, 4))
            hi, low = split(v)
            f2[s // 4, here, i * BS : (i + 1) * BS] = hi
            f2[s // 4, here, (4 + i) * BS : (5 + i) * BS] = low
            hi, low = split(v.T)
            half = slice(i % 2 * BS, (i % 2 + 1) * BS)
            ft2[i // 2, half, rows(s)] = hi
            ft2[i // 2, half, rows(8 + s)] = low

    load_m.wait()
    tiles(0)
    for j in (1, 7):
        over_z(j).wait_recv()
        over_y(j)
    tiles(1)
    for j in (2, 6, 3, 5):
        over_z(j).wait_recv()
        over_y(j)
    v = pinv[...]
    p2[...] = pair_of(v)
    pt2[...] = pair_of(v.T)
    over_z(4).wait_recv()
    over_y(4)
    tiles(2)
    tiles(3)
    for t in range(N):
        load_r(t).wait()
        load_p(t).wait()
    for j in range(8):
        for way in (1, 2, 3):
            piece(j, way).wait_recv()

    @pl.loop(0, 4)
    def _(i):
        v = inv_all[i]
        i2[i] = pair_of(v)
        it2[i] = pair_of(v.T)

    def forward(t):
        @pl.loop(0, 4)
        def _(i):
            b = pair_of(dot1(i2[i], pair_of(t_all[t, i])))
            l2[rows(i), :] = b
            l2[rows(4 + i), :] = b

        d_all[t] = dot1(it2[y, mine], l2[rows(y), :])
        @pl.loop(0, 2)
        def _(n):
            core = lax.rem(1 - k + n, 2)
            u_all[t, core] = dot2(f2[core], l2[...])

            @pl.when(n == 0)
            def _():
                start(t, PAIR)

    def add(ref, at, other):
        ref[at] = ref[at] + other

    def stage1(t):
        arrived(t, PAIR)
        u, got = u_all.at[t, k], pair.at[t]
        add(u, rows(xo), got[rows(xo)])
        start(t, XA, XB)
        add(u, rows(xp), got[rows(xp)])
        add(u, rows(xm), got[rows(xm)])
        start(t, MB, PA)
        add(u, rows(x), got[rows(x)])

    def stage2(t):
        arrived(t, XA)
        add(u_all.at[t, k], rows(xp, 0, HB), xa[t])
        start(t, MA)
        arrived(t, XB)
        add(u_all.at[t, k], rows(xm, HB, HB), xb[t])
        start(t, PB)

    def keep(t):
        return pltpu.make_async_copy(s_all.at[t, own + x], out_p.at[:, pl.ds(t * W, W)], out_sem.at[t])

    def solve(t):
        arrived(t, MA, MB, PA, PB)
        v = res[t] - ((u_all[t, k, rows(x)] + ym[t]) + yp[t])
        v = dot1(p2[...], pair_of(v))
        s_all[t, own + x] = dot1(pt2[...], pair_of(v))
        start(t, GP, GM, GC)
        keep(t).start()

    def relay(t):
        arrived(t, GP)
        start(t, HA, FM)
        arrived(t, GM)
        start(t, HBK, FP)

    def opposite(t):
        arrived(t, HA, HBK)
        start(t, FO)

    def backward(t):
        arrived(t, GC, FM, FP, FO)

        @pl.loop(0, 8)
        def _(s):
            b = pair_of(s_all[t, s])
            s2[rows(s), :] = b
            s2[rows(8 + s), :] = b

        @pl.loop(0, 2)
        def _(i):
            v = dot2(ft2[i], s2[...])
            t_all[t, 2 * i] = dot1(it2[2 * i], pair_of(v[:BS]))
            t_all[t, 2 * i + 1] = dot1(it2[2 * i + 1], pair_of(v[BS:]))

        start(t, YXA, YXB, YMB, YPA)

    def y_stage2(t):
        arrived(t, YXA)
        t_all[t, yp_i, lo] = t_all[t, yp_i, lo] + yxa[t]
        start(t, YMA)
        arrived(t, YXB)
        t_all[t, ym_i, up] = t_all[t, ym_i, up] + yxb[t]
        start(t, YPB)

    def z_send(t):
        arrived(t, YMA, YMB, YPA, YPB)
        t_all[t, y] = (t_all[t, y] + yym[t]) + yyp[t]
        start(t, *range(Z1, Z1 + 7))

    def finish(t):
        arrived(t, *range(Z1, Z1 + 7))
        total = t_all[t, y, mine]
        for j in range(7):
            total = total + zr[t, j]
        out_l[:, pl.ds(pl.multiple_of(t * W, W), W)] = d_all[t] - total
        keep(t).wait()
        for kind in range(KINDS):
            copy(kind, t).wait_send()

    stages = dict(
        forward=forward, stage1=stage1, stage2=stage2, solve=solve, relay=relay, opposite=opposite,
        backward=backward, y_stage2=y_stage2, z_send=z_send, finish=finish,
    )

    @pl.loop(0, N + max(lag for _, lag in ORDER))
    def _(step):
        for name, lag in ORDER:
            t = step - lag

            @pl.when(jnp.logical_and(t >= 0, t < N))
            def _():
                stages[name](t)

    for j in range(8):
        for way in range(4):
            if j or way:
                (piece(j, way) if way else over_z(j)).wait_send()


def hand_on(solved, leaf, out_p, out_l):
    out_p[...] = solved[...]
    out_l[...] = leaf[...]


def body(leaf_rhs, leaf_inverse, parent_rhs, parent_inverse, factor, tile_mask):
    vmem = pl.BlockSpec(memory_space=pltpu.VMEM)
    hbm = pl.BlockSpec(memory_space=pl.ANY)
    f32, b16 = (lambda *s: pltpu.VMEM(s, F32)), (lambda *s: pltpu.VMEM(s, BF16))
    dma = lambda *s: pltpu.SemaphoreType.DMA(s)
    solved, leaf = pl.pallas_call(
        kernel,
        out_shape=(
            jax.ShapeDtypeStruct((BS, N * W), F32),
            jax.ShapeDtypeStruct((ROWS, N * W), F32),
        ),
        in_specs=[hbm, hbm, vmem, hbm, vmem, hbm],
        out_specs=(hbm, vmem),
        scratch_shapes=[
            b16(2, 4 * BS, 8 * BS),
            b16(2, 2 * BS, 16 * BS),
            f32(N, 8, BS, W),
            f32(N, 4, BS, W),
            f32(N, 2, 4 * BS, W),
            f32(N, 4 * BS, W),
            f32(N, HB, W), f32(N, HB, W),
            f32(N, BS, W), f32(N, BS, W),
            f32(N, HB, W), f32(N, HB, W),
            f32(N, BS, W), f32(N, BS, W),
            f32(N, 7, ROWS, W),
            f32(4, BS, BS),
            b16(4, BS, 2 * BS), b16(4, BS, 2 * BS),
            b16(8 * BS, 2 * W),
            b16(16 * BS, 2 * W),
            f32(N, BS, W),
            b16(BS, 2 * BS), b16(BS, 2 * BS),
            f32(N, ROWS, W),
            pltpu.SMEM((1, 4, 8), jnp.int32),
            dma(3 * N + 1), dma(N), dma(8, 4), dma(8, 4), dma(N, KINDS), dma(N, KINDS),
        ],
        compiler_params=pltpu.CompilerParams(
            collective_id=0, has_side_effects=True, vmem_limit_bytes=63 * 2**20
        ),
    )(
        jnp.swapaxes(tile_mask, 1, 2),
        leaf_rhs.reshape(4, BS, N * W),
        leaf_inverse,
        parent_rhs[0],
        parent_inverse[0],
        factor[0].reshape(8, BS, 4 * BS),
    )
    solved, leaf = pl.pallas_call(
        hand_on,
        out_shape=(
            jax.ShapeDtypeStruct((BS, N * W), F32),
            jax.ShapeDtypeStruct((ROWS, N * W), F32),
        ),
        in_specs=[vmem, vmem],
        out_specs=(vmem, vmem),
    )(solved, leaf)
    return solved[None], leaf


def solution(mesh):
    placed = (
        P("prow", None),
        P(("prow", "pcol"), None),
        P("pcol", "prow", None),
        P("pcol", "prow", None),
        P("pcol", None, "prow"),
        P("pcol", None, "prow"),
    )
    return jax.shard_map(
        body,
        mesh=mesh,
        in_specs=placed,
        out_specs=(P("pcol", "prow", None), P(("prow", "pcol"), None)),
        check_vma=False,
    )
```

```python
import jax
import jax.numpy as jnp
from jax import lax
from jax.experimental import pallas as pl
from jax.experimental.pallas import tpu as pltpu
from jax.sharding import PartitionSpec as P

MESH = pl.DeviceIdType.MESH
F32 = jnp.float32
BF16 = jnp.bfloat16
BS = 256
W = 128
N = 8
HB = BS // 2
ROWS = 32

(PAIR, XA, XB, MB, MA, PA, PB, GP, GM, GC, HA, HBK, FM, FP, FO, YXA, YXB, YMB, YMA, YPA, YPB, Z1) = range(22)
KINDS = Z1 + 7


def split(v):
    hi = v.astype(BF16)
    return hi, (v - hi.astype(F32)).astype(BF16)


def dot(a, b):
    return jnp.dot(a, b, preferred_element_type=F32)


def pair_of(v):
    return jnp.concatenate(split(v), axis=1)


def dot2(a, b):
    r = dot(a, b)
    return r[:, :W] + r[:, W:]


def dot1(a, b):
    return dot2(a, jnp.concatenate([b, b], axis=0))


ORDER = (
    ("forward", 0), ("opposite", 6), ("relay", 5), ("stage1", 0), ("z_send", 10),
    ("y_stage2", 8), ("solve", 3), ("finish", 13), ("stage2", 1), ("backward", 6),
)


def kernel(
    mask_in, rhs, inv, prhs, pinv, fac, out_p, out_l,
    f2, ft2, s_all, t_all, u_all, pair, xa, xb, ym, yp, yxa, yxb, yym, yyp, zr,
    inv_all, i2, it2, l2, s2, res, p2, pt2, d_all, mask,
    load_sem, out_sem, a_send, a_recv, send, recv,
):
    p = lax.axis_index("prow")
    q = lax.axis_index("pcol")
    x, k = p // 2, lax.rem(p, 2)
    y, z = q // 8, lax.rem(q, 8)
    xp, xm, xo = lax.rem(x + 1, 4), lax.rem(x + 3, 4), lax.rem(x + 2, 4)
    yp_i, ym_i, yo = lax.rem(y + 1, 4), lax.rem(y + 3, 4), lax.rem(y + 2, 4)
    dev_c = (x * 2 + 1 - k, q)
    dev_xp, dev_xm = (xp * 2 + k, q), (xm * 2 + k, q)
    dev_yp, dev_ym = (p, yp_i * 8 + z), (p, ym_i * 8 + z)

    def z_at(j):
        return lax.rem(z + j, 8)

    def dev_z(j):
        return (p, y * 8 + z_at(j))

    def dev_y(j):
        return (p, lax.rem(y + j, 4) * 8 + z)

    lo, up = pl.ds(0, HB), pl.ds(HB, HB)
    own = k * 4

    def rows(at, start=0, size=BS):
        return pl.ds(pl.multiple_of(at * BS + start, HB), size)

    def copy(kind, t):
        def go(src, dst, dev):
            return pltpu.make_async_remote_copy(
                src_ref=src, dst_ref=dst, send_sem=send.at[t, kind], recv_sem=recv.at[t, kind],
                device_id=dev, device_id_type=MESH,
            )

        if kind == PAIR:
            return go(u_all.at[t, 1 - k], pair.at[t], dev_c)
        if kind == XA:
            return go(u_all.at[t, k, rows(xo, 0, HB)], xa.at[t], dev_xp)
        if kind == XB:
            return go(u_all.at[t, k, rows(xo, HB, HB)], xb.at[t], dev_xm)
        if kind == MB:
            return go(u_all.at[t, k, rows(xp, HB, HB)], ym.at[t, up], dev_xp)
        if kind == MA:
            return go(u_all.at[t, k, rows(xp, 0, HB)], ym.at[t, lo], dev_xp)
        if kind == PA:
            return go(u_all.at[t, k, rows(xm, 0, HB)], yp.at[t, lo], dev_xm)
        if kind == PB:
            return go(u_all.at[t, k, rows(xm, HB, HB)], yp.at[t, up], dev_xm)
        if kind in (GP, GM, GC):
            ref = s_all.at[t, own + x]
            return go(ref, ref, {GP: dev_xp, GM: dev_xm, GC: dev_c}[kind])
        if kind == HA:
            ref = s_all.at[t, own + xm, lo]
            return go(ref, ref, dev_xp)
        if kind == HBK:
            ref = s_all.at[t, own + xp, up]
            return go(ref, ref, dev_xm)
        if kind in (FM, FP, FO):
            ref = s_all.at[t, own + {FM: xm, FP: xp, FO: xo}[kind]]
            return go(ref, ref, dev_c)
        if kind == YXA:
            return go(t_all.at[t, yo, lo], yxa.at[t], dev_yp)
        if kind == YXB:
            return go(t_all.at[t, yo, up], yxb.at[t], dev_ym)
        if kind == YMB:
            return go(t_all.at[t, yp_i, up], yym.at[t, up], dev_yp)
        if kind == YMA:
            return go(t_all.at[t, yp_i, lo], yym.at[t, lo], dev_yp)
        if kind == YPA:
            return go(t_all.at[t, ym_i, lo], yyp.at[t, lo], dev_ym)
        if kind == YPB:
            return go(t_all.at[t, ym_i, up], yyp.at[t, up], dev_ym)
        j = kind - Z1 + 1
        return go(t_all.at[t, y, pl.ds(z_at(j) * ROWS, ROWS)], zr.at[t, j - 1], dev_z(j))

    def start(t, *kinds):
        for kind in kinds:
            copy(kind, t).start()

    def arrived(t, *kinds):
        for kind in kinds:
            copy(kind, t).wait_recv()

    def load_f(i):
        return pltpu.make_async_copy(
            fac.at[:, :, pl.ds(i * W, W)], s_all.at[i], load_sem.at[i]
        )

    def load_r(t):
        return pltpu.make_async_copy(
            rhs.at[:, :, pl.ds(t * W, W)], t_all.at[t], load_sem.at[N + t]
        )

    def load_p(t):
        return pltpu.make_async_copy(
            prhs.at[:, pl.ds(t * W, W)], res.at[t], load_sem.at[2 * N + t]
        )

    load_m = pltpu.make_async_copy(mask_in, mask, load_sem.at[3 * N])
    load_m.start()
    for i in range(N):
        load_f(i).start()
    for t in range(N):
        load_r(t).start()
    for t in range(N):
        load_p(t).start()

    barrier = pltpu.get_barrier_semaphore()
    others = [dev_c, dev_xp, dev_xm]
    others += [dev_y(j) for j in range(1, 4)] + [dev_z(j) for j in range(1, 8)]
    for dev in others:
        pl.semaphore_signal(barrier, inc=1, device_id=dev, device_id_type=MESH)
    mine = pl.ds(pl.multiple_of(z * ROWS, ROWS), ROWS)
    inv_all[y, mine, :] = inv[...]
    pl.semaphore_wait(barrier, len(others))

    def piece(j, way):
        at = pl.ds(pl.multiple_of(lax.rem(z + 8 - j, 8) * ROWS, ROWS), ROWS)
        ref = inv_all.at[y, at]
        return pltpu.make_async_remote_copy(
            src_ref=ref, dst_ref=ref, send_sem=a_send.at[j, way], recv_sem=a_recv.at[j, way],
            device_id=dev_y(way) if way else dev_z(j), device_id_type=MESH,
        )

    def over_y(j):
        for way in (1, 3, 2):
            piece(j, way).start()

    def over_z(j):
        return pltpu.make_async_remote_copy(
            src_ref=inv_all.at[y, mine], dst_ref=inv_all.at[y, mine],
            send_sem=a_send.at[j, 0], recv_sem=a_recv.at[j, 0],
            device_id=dev_z(j), device_id_type=MESH,
        )

    for j in (1, 7, 2, 6, 3, 5, 4):
        over_z(j).start()
    over_y(0)

    def tiles(i):
        load_f(2 * i).wait()
        load_f(2 * i + 1).wait()

        @pl.loop(0, 8)
        def _(s):
            r = lax.rem(s, 4) * 2 + s // 4
            v = jnp.concatenate([s_all[2 * i, r], s_all[2 * i + 1, r]], axis=1)
            v = v * mask[0, i, r].astype(F32)
            here = rows(lax.rem(s, 4))
            hi, low = split(v)
            f2[s // 4, here, i * BS : (i + 1) * BS] = hi
            f2[s // 4, here, (4 + i) * BS : (5 + i) * BS] = low
            hi, low = split(v.T)
            half = slice(i % 2 * BS, (i % 2 + 1) * BS)
            ft2[i // 2, half, rows(s)] = hi
            ft2[i // 2, half, rows(8 + s)] = low

    load_m.wait()
    tiles(0)
    for j in (1, 7):
        over_z(j).wait_recv()
        over_y(j)
    tiles(1)
    for j in (2, 6, 3, 5):
        over_z(j).wait_recv()
        over_y(j)
    v = pinv[...]
    p2[...] = pair_of(v)
    pt2[...] = pair_of(v.T)
    over_z(4).wait_recv()
    over_y(4)
    tiles(2)
    tiles(3)
    for t in range(N):
        load_r(t).wait()
        load_p(t).wait()
    for j in range(8):
        for way in (1, 2, 3):
            piece(j, way).wait_recv()

    @pl.loop(0, 4)
    def _(i):
        v = inv_all[i]
        i2[i] = pair_of(v)
        it2[i] = pair_of(v.T)

    def forward(t):
        @pl.loop(0, 4)
        def _(i):
            b = pair_of(dot1(i2[i], pair_of(t_all[t, i])))
            l2[rows(i), :] = b
            l2[rows(4 + i), :] = b

        d_all[t] = dot1(it2[y, mine], l2[rows(y), :])
        @pl.loop(0, 2)
        def _(n):
            core = lax.rem(1 - k + n, 2)
            u_all[t, core] = dot2(f2[core], l2[...])

            @pl.when(n == 0)
            def _():
                start(t, PAIR)

    def add(ref, at, other):
        ref[at] = ref[at] + other

    def stage1(t):
        arrived(t, PAIR)
        u, got = u_all.at[t, k], pair.at[t]
        add(u, rows(xo), got[rows(xo)])
        start(t, XA, XB)
        add(u, rows(xp), got[rows(xp)])
        add(u, rows(xm), got[rows(xm)])
        start(t, MB, PA)
        add(u, rows(x), got[rows(x)])

    def stage2(t):
        arrived(t, XA)
        add(u_all.at[t, k], rows(xp, 0, HB), xa[t])
        start(t, MA)
        arrived(t, XB)
        add(u_all.at[t, k], rows(xm, HB, HB), xb[t])
        start(t, PB)

    def keep(t):
        return pltpu.make_async_copy(s_all.at[t, own + x], out_p.at[:, pl.ds(t * W, W)], out_sem.at[t])

    def solve(t):
        arrived(t, MA, MB, PA, PB)
        v = res[t] - ((u_all[t, k, rows(x)] + ym[t]) + yp[t])
        v = dot1(p2[...], pair_of(v))
        s_all[t, own + x] = dot1(pt2[...], pair_of(v))
        start(t, GP, GM, GC)
        keep(t).start()

    def relay(t):
        arrived(t, GP)
        start(t, HA, FM)
        arrived(t, GM)
        start(t, HBK, FP)

    def opposite(t):
        arrived(t, HA, HBK)
        start(t, FO)

    def backward(t):
        arrived(t, GC, FM, FP, FO)

        @pl.loop(0, 8)
        def _(s):
            b = pair_of(s_all[t, s])
            s2[rows(s), :] = b
            s2[rows(8 + s), :] = b

        @pl.loop(0, 2)
        def _(n):
            i = lax.rem(yo // 2 + n, 2)
            v = dot2(ft2[i], s2[...])
            t_all[t, 2 * i] = dot1(it2[2 * i], pair_of(v[:BS]))
            t_all[t, 2 * i + 1] = dot1(it2[2 * i + 1], pair_of(v[BS:]))

            @pl.when(n == 0)
            def _():
                start(t, YXA, YXB)

        start(t, YMB, YPA)

    def y_stage2(t):
        arrived(t, YXA)
        t_all[t, yp_i, lo] = t_all[t, yp_i, lo] + yxa[t]
        start(t, YMA)
        arrived(t, YXB)
        t_all[t, ym_i, up] = t_all[t, ym_i, up] + yxb[t]
        start(t, YPB)

    def z_send(t):
        arrived(t, YMA, YMB, YPA, YPB)
        t_all[t, y] = (t_all[t, y] + yym[t]) + yyp[t]
        start(t, *range(Z1, Z1 + 7))

    def finish(t):
        arrived(t, *range(Z1, Z1 + 7))
        total = t_all[t, y, mine]
        for j in range(7):
            total = total + zr[t, j]
        out_l[:, pl.ds(pl.multiple_of(t * W, W), W)] = d_all[t] - total
        keep(t).wait()
        for kind in range(KINDS):
            copy(kind, t).wait_send()

    stages = dict(
        forward=forward, stage1=stage1, stage2=stage2, solve=solve, relay=relay, opposite=opposite,
        backward=backward, y_stage2=y_stage2, z_send=z_send, finish=finish,
    )

    @pl.loop(0, N + max(lag for _, lag in ORDER))
    def _(step):
        for name, lag in ORDER:
            t = step - lag

            @pl.when(jnp.logical_and(t >= 0, t < N))
            def _():
                stages[name](t)

    for j in range(8):
        for way in range(4):
            if j or way:
                (piece(j, way) if way else over_z(j)).wait_send()


def hand_on(solved, leaf, out_p, out_l):
    out_p[...] = solved[...]
    out_l[...] = leaf[...]


def body(leaf_rhs, leaf_inverse, parent_rhs, parent_inverse, factor, tile_mask):
    vmem = pl.BlockSpec(memory_space=pltpu.VMEM)
    hbm = pl.BlockSpec(memory_space=pl.ANY)
    f32, b16 = (lambda *s: pltpu.VMEM(s, F32)), (lambda *s: pltpu.VMEM(s, BF16))
    dma = lambda *s: pltpu.SemaphoreType.DMA(s)
    solved, leaf = pl.pallas_call(
        kernel,
        out_shape=(
            jax.ShapeDtypeStruct((BS, N * W), F32),
            jax.ShapeDtypeStruct((ROWS, N * W), F32),
        ),
        in_specs=[hbm, hbm, vmem, hbm, vmem, hbm],
        out_specs=(hbm, vmem),
        scratch_shapes=[
            b16(2, 4 * BS, 8 * BS),
            b16(2, 2 * BS, 16 * BS),
            f32(N, 8, BS, W),
            f32(N, 4, BS, W),
            f32(N, 2, 4 * BS, W),
            f32(N, 4 * BS, W),
            f32(N, HB, W), f32(N, HB, W),
            f32(N, BS, W), f32(N, BS, W),
            f32(N, HB, W), f32(N, HB, W),
            f32(N, BS, W), f32(N, BS, W),
            f32(N, 7, ROWS, W),
            f32(4, BS, BS),
            b16(4, BS, 2 * BS), b16(4, BS, 2 * BS),
            b16(8 * BS, 2 * W),
            b16(16 * BS, 2 * W),
            f32(N, BS, W),
            b16(BS, 2 * BS), b16(BS, 2 * BS),
            f32(N, ROWS, W),
            pltpu.SMEM((1, 4, 8), jnp.int32),
            dma(3 * N + 1), dma(N), dma(8, 4), dma(8, 4), dma(N, KINDS), dma(N, KINDS),
        ],
        compiler_params=pltpu.CompilerParams(
            collective_id=0, has_side_effects=True, vmem_limit_bytes=63 * 2**20
        ),
    )(
        jnp.swapaxes(tile_mask, 1, 2),
        leaf_rhs.reshape(4, BS, N * W),
        leaf_inverse,
        parent_rhs[0],
        parent_inverse[0],
        factor[0].reshape(8, BS, 4 * BS),
    )
    solved, leaf = pl.pallas_call(
        hand_on,
        out_shape=(
            jax.ShapeDtypeStruct((BS, N * W), F32),
            jax.ShapeDtypeStruct((ROWS, N * W), F32),
        ),
        in_specs=[vmem, vmem],
        out_specs=(vmem, vmem),
    )(solved, leaf)
    return solved[None], leaf


def solution(mesh):
    placed = (
        P("prow", None),
        P(("prow", "pcol"), None),
        P("pcol", "prow", None),
        P("pcol", "prow", None),
        P("pcol", None, "prow"),
        P("pcol", None, "prow"),
    )
    return jax.shard_map(
        body,
        mesh=mesh,
        in_specs=placed,
        out_specs=(P("pcol", "prow", None), P(("prow", "pcol"), None)),
        check_vma=False,
    )
```

```python
import jax
import jax.numpy as jnp
from jax import lax
from jax.experimental import pallas as pl
from jax.experimental.pallas import tpu as pltpu
from jax.sharding import PartitionSpec as P

MESH = pl.DeviceIdType.MESH
F32 = jnp.float32
BF16 = jnp.bfloat16
BS = 256
W = 128
N = 8
HB = BS // 2
ROWS = 32

(PAIR, XA, XB, MB, MA, PA, PB, GP, GM, GC, HA, HBK, FM, FP, FO, YXA, YXB, YMB, YMA, YPA, YPB, Z1) = range(22)
KINDS = Z1 + 7
SHARED = {MB: MA, PB: PA, YMB: YMA, YPB: YPA, FM: GC, FP: GC, FO: GC}
SHARED.update({Z1 + j: Z1 for j in range(1, 7)})


def split(v):
    hi = v.astype(BF16)
    return hi, (v - hi.astype(F32)).astype(BF16)


def dot(a, b):
    return jnp.dot(a, b, preferred_element_type=F32)


def pair_of(v):
    return jnp.concatenate(split(v), axis=1)


def dot2(a, b):
    r = dot(a, b)
    return r[:, :W] + r[:, W:]


def dot1(a, b):
    return dot2(a, jnp.concatenate([b, b], axis=0))


ORDER = (
    ("forward", 0), ("opposite", 6), ("relay", 5), ("stage1", 0), ("z_send", 10),
    ("y_stage2", 8), ("solve", 3), ("finish", 13), ("stage2", 1), ("backward", 6),
)


def kernel(
    mask_in, rhs, inv, prhs, pinv, fac, out_p, out_l,
    f2, ft2, s_all, t_all, u_all, pair, xa, xb, ym, yp, yxa, yxb, yym, yyp, zr,
    inv_all, i2, it2, l2, s2, res, p2, pt2, d_all, mask,
    load_sem, out_sem, a_send, a_recv, send, recv,
):
    p = lax.axis_index("prow")
    q = lax.axis_index("pcol")
    x, k = p // 2, lax.rem(p, 2)
    y, z = q // 8, lax.rem(q, 8)
    xp, xm, xo = lax.rem(x + 1, 4), lax.rem(x + 3, 4), lax.rem(x + 2, 4)
    yp_i, ym_i, yo = lax.rem(y + 1, 4), lax.rem(y + 3, 4), lax.rem(y + 2, 4)
    dev_c = (x * 2 + 1 - k, q)
    dev_xp, dev_xm = (xp * 2 + k, q), (xm * 2 + k, q)
    dev_yp, dev_ym = (p, yp_i * 8 + z), (p, ym_i * 8 + z)

    def z_at(j):
        return lax.rem(z + j, 8)

    def dev_z(j):
        return (p, y * 8 + z_at(j))

    def dev_y(j):
        return (p, lax.rem(y + j, 4) * 8 + z)

    lo, up = pl.ds(0, HB), pl.ds(HB, HB)
    own = k * 4

    def rows(at, start=0, size=BS):
        return pl.ds(pl.multiple_of(at * BS + start, HB), size)

    def copy(kind, t):
        sem = SHARED.get(kind, kind)

        def go(src, dst, dev):
            return pltpu.make_async_remote_copy(
                src_ref=src, dst_ref=dst, send_sem=send.at[t, sem], recv_sem=recv.at[t, sem],
                device_id=dev, device_id_type=MESH,
            )

        if kind == PAIR:
            return go(u_all.at[t, 1 - k], pair.at[t], dev_c)
        if kind == XA:
            return go(u_all.at[t, k, rows(xo, 0, HB)], xa.at[t], dev_xp)
        if kind == XB:
            return go(u_all.at[t, k, rows(xo, HB, HB)], xb.at[t], dev_xm)
        if kind == MB:
            return go(u_all.at[t, k, rows(xp, HB, HB)], ym.at[t, up], dev_xp)
        if kind == MA:
            return go(u_all.at[t, k, rows(xp, 0, HB)], ym.at[t, lo], dev_xp)
        if kind == PA:
            return go(u_all.at[t, k, rows(xm, 0, HB)], yp.at[t, lo], dev_xm)
        if kind == PB:
            return go(u_all.at[t, k, rows(xm, HB, HB)], yp.at[t, up], dev_xm)
        if kind in (GP, GM, GC):
            ref = s_all.at[t, own + x]
            return go(ref, ref, {GP: dev_xp, GM: dev_xm, GC: dev_c}[kind])
        if kind == HA:
            ref = s_all.at[t, own + xm, lo]
            return go(ref, ref, dev_xp)
        if kind == HBK:
            ref = s_all.at[t, own + xp, up]
            return go(ref, ref, dev_xm)
        if kind in (FM, FP, FO):
            ref = s_all.at[t, own + {FM: xm, FP: xp, FO: xo}[kind]]
            return go(ref, ref, dev_c)
        if kind == YXA:
            return go(t_all.at[t, yo, lo], yxa.at[t], dev_yp)
        if kind == YXB:
            return go(t_all.at[t, yo, up], yxb.at[t], dev_ym)
        if kind == YMB:
            return go(t_all.at[t, yp_i, up], yym.at[t, up], dev_yp)
        if kind == YMA:
            return go(t_all.at[t, yp_i, lo], yym.at[t, lo], dev_yp)
        if kind == YPA:
            return go(t_all.at[t, ym_i, lo], yyp.at[t, lo], dev_ym)
        if kind == YPB:
            return go(t_all.at[t, ym_i, up], yyp.at[t, up], dev_ym)
        j = kind - Z1 + 1
        return go(t_all.at[t, y, pl.ds(z_at(j) * ROWS, ROWS)], zr.at[t, j - 1], dev_z(j))

    def start(t, *kinds):
        for kind in kinds:
            copy(kind, t).start()

    def whole(kind, t):
        ref = None
        if kind in (MA, PA, YMA, YPA):
            ref = {MA: ym, PA: yp, YMA: yym, YPA: yyp}[kind].at[t]
        if kind == GC:
            ref = s_all.at[t, pl.ds((1 - k) * 4, 4)]
        if kind == Z1:
            ref = zr.at[t]
        if ref is None:
            return copy(kind, t)
        return pltpu.make_async_remote_copy(
            src_ref=ref, dst_ref=ref, send_sem=send.at[t, kind], recv_sem=recv.at[t, kind],
            device_id=dev_c, device_id_type=MESH,
        )

    def arrived(t, *kinds):
        for kind in kinds:
            whole(kind, t).wait_recv()

    def load_f(i):
        return pltpu.make_async_copy(
            fac.at[:, :, pl.ds(i * W, W)], s_all.at[i], load_sem.at[i]
        )

    def load_r(t):
        return pltpu.make_async_copy(
            rhs.at[:, :, pl.ds(t * W, W)], t_all.at[t], load_sem.at[N + t]
        )

    def load_p(t):
        return pltpu.make_async_copy(
            prhs.at[:, pl.ds(t * W, W)], res.at[t], load_sem.at[2 * N + t]
        )

    load_m = pltpu.make_async_copy(mask_in, mask, load_sem.at[3 * N])
    load_m.start()
    for i in range(N):
        load_f(i).start()
    for t in range(N):
        load_r(t).start()
    for t in range(N):
        load_p(t).start()

    barrier = pltpu.get_barrier_semaphore()
    others = [dev_c, dev_xp, dev_xm]
    others += [dev_y(j) for j in range(1, 4)] + [dev_z(j) for j in range(1, 8)]
    for dev in others:
        pl.semaphore_signal(barrier, inc=1, device_id=dev, device_id_type=MESH)
    mine = pl.ds(pl.multiple_of(z * ROWS, ROWS), ROWS)
    inv_all[y, mine, :] = inv[...]
    pl.semaphore_wait(barrier, len(others))

    def piece(j, way):
        at = pl.ds(pl.multiple_of(lax.rem(z + 8 - j, 8) * ROWS, ROWS), ROWS)
        ref = inv_all.at[y, at]
        return pltpu.make_async_remote_copy(
            src_ref=ref, dst_ref=ref, send_sem=a_send.at[j, way], recv_sem=a_recv.at[j, way],
            device_id=dev_y(way) if way else dev_z(j), device_id_type=MESH,
        )

    def over_y(j):
        for way in (1, 3, 2):
            piece(j, way).start()

    def over_z(j):
        return pltpu.make_async_remote_copy(
            src_ref=inv_all.at[y, mine], dst_ref=inv_all.at[y, mine],
            send_sem=a_send.at[j, 0], recv_sem=a_recv.at[j, 0],
            device_id=dev_z(j), device_id_type=MESH,
        )

    for j in (1, 7, 2, 6, 3, 5, 4):
        over_z(j).start()
    over_y(0)

    def tiles(i):
        load_f(2 * i).wait()
        load_f(2 * i + 1).wait()

        @pl.loop(0, 8)
        def _(s):
            r = lax.rem(s, 4) * 2 + s // 4
            v = jnp.concatenate([s_all[2 * i, r], s_all[2 * i + 1, r]], axis=1)
            v = v * mask[0, i, r].astype(F32)
            here = rows(lax.rem(s, 4))
            hi, low = split(v)
            f2[s // 4, here, i * BS : (i + 1) * BS] = hi
            f2[s // 4, here, (4 + i) * BS : (5 + i) * BS] = low
            hi, low = split(v.T)
            half = slice(i % 2 * BS, (i % 2 + 1) * BS)
            ft2[i // 2, half, rows(s)] = hi
            ft2[i // 2, half, rows(8 + s)] = low

    load_m.wait()
    tiles(0)
    for j in (1, 7):
        over_z(j).wait_recv()
        over_y(j)
    tiles(1)
    for j in (2, 6, 3, 5):
        over_z(j).wait_recv()
        over_y(j)
    v = pinv[...]
    p2[...] = pair_of(v)
    pt2[...] = pair_of(v.T)
    over_z(4).wait_recv()
    over_y(4)
    tiles(2)
    tiles(3)
    for t in range(N):
        load_r(t).wait()
        load_p(t).wait()
    for j in range(8):
        for way in (1, 2, 3):
            piece(j, way).wait_recv()

    @pl.loop(0, 4)
    def _(i):
        v = inv_all[i]
        i2[i] = pair_of(v)
        it2[i] = pair_of(v.T)

    def forward(t):
        @pl.loop(0, 4)
        def _(i):
            b = pair_of(dot1(i2[i], pair_of(t_all[t, i])))
            l2[rows(i), :] = b
            l2[rows(4 + i), :] = b

        d_all[t] = dot1(it2[y, mine], l2[rows(y), :])
        @pl.loop(0, 2)
        def _(n):
            core = lax.rem(1 - k + n, 2)
            u_all[t, core] = dot2(f2[core], l2[...])

            @pl.when(n == 0)
            def _():
                start(t, PAIR)

    def add(ref, at, other):
        ref[at] = ref[at] + other

    def stage1(t):
        arrived(t, PAIR)
        u, got = u_all.at[t, k], pair.at[t]
        add(u, rows(xo), got[rows(xo)])
        start(t, XA, XB)
        add(u, rows(xp), got[rows(xp)])
        add(u, rows(xm), got[rows(xm)])
        start(t, MB, PA)
        add(u, rows(x), got[rows(x)])

    def stage2(t):
        arrived(t, XA)
        add(u_all.at[t, k], rows(xp, 0, HB), xa[t])
        start(t, MA)
        arrived(t, XB)
        add(u_all.at[t, k], rows(xm, HB, HB), xb[t])
        start(t, PB)

    def keep(t):
        return pltpu.make_async_copy(s_all.at[t, own + x], out_p.at[:, pl.ds(t * W, W)], out_sem.at[t])

    def solve(t):
        arrived(t, MA, PA)
        v = res[t] - ((u_all[t, k, rows(x)] + ym[t]) + yp[t])
        v = dot1(p2[...], pair_of(v))
        s_all[t, own + x] = dot1(pt2[...], pair_of(v))
        start(t, GP, GM, GC)
        keep(t).start()

    def relay(t):
        arrived(t, GP)
        start(t, HA, FM)
        arrived(t, GM)
        start(t, HBK, FP)

    def opposite(t):
        arrived(t, HA, HBK)
        start(t, FO)

    def backward(t):
        arrived(t, GC)

        @pl.loop(0, 8)
        def _(s):
            b = pair_of(s_all[t, s])
            s2[rows(s), :] = b
            s2[rows(8 + s), :] = b

        @pl.loop(0, 2)
        def _(n):
            i = lax.rem(yo // 2 + n, 2)
            v = dot2(ft2[i], s2[...])
            t_all[t, 2 * i] = dot1(it2[2 * i], pair_of(v[:BS]))
            t_all[t, 2 * i + 1] = dot1(it2[2 * i + 1], pair_of(v[BS:]))

            @pl.when(n == 0)
            def _():
                start(t, YXA, YXB)

        start(t, YMB, YPA)

    def y_stage2(t):
        arrived(t, YXA)
        t_all[t, yp_i, lo] = t_all[t, yp_i, lo] + yxa[t]
        start(t, YMA)
        arrived(t, YXB)
        t_all[t, ym_i, up] = t_all[t, ym_i, up] + yxb[t]
        start(t, YPB)

    def z_send(t):
        arrived(t, YMA, YPA)
        t_all[t, y] = (t_all[t, y] + yym[t]) + yyp[t]
        start(t, *range(Z1, Z1 + 7))

    def finish(t):
        arrived(t, Z1)
        total = t_all[t, y, mine]
        for j in range(7):
            total = total + zr[t, j]
        out_l[:, pl.ds(pl.multiple_of(t * W, W), W)] = d_all[t] - total
        keep(t).wait()
        for kind in range(KINDS):
            if kind not in SHARED:
                whole(kind, t).wait_send()

    stages = dict(
        forward=forward, stage1=stage1, stage2=stage2, solve=solve, relay=relay, opposite=opposite,
        backward=backward, y_stage2=y_stage2, z_send=z_send, finish=finish,
    )

    @pl.loop(0, N + max(lag for _, lag in ORDER))
    def _(step):
        for name, lag in ORDER:
            t = step - lag

            @pl.when(jnp.logical_and(t >= 0, t < N))
            def _():
                stages[name](t)

    for j in range(8):
        for way in range(4):
            if j or way:
                (piece(j, way) if way else over_z(j)).wait_send()


def hand_on(solved, leaf, out_p, out_l):
    out_p[...] = solved[...]
    out_l[...] = leaf[...]


def body(leaf_rhs, leaf_inverse, parent_rhs, parent_inverse, factor, tile_mask):
    vmem = pl.BlockSpec(memory_space=pltpu.VMEM)
    hbm = pl.BlockSpec(memory_space=pl.ANY)
    f32, b16 = (lambda *s: pltpu.VMEM(s, F32)), (lambda *s: pltpu.VMEM(s, BF16))
    dma = lambda *s: pltpu.SemaphoreType.DMA(s)
    solved, leaf = pl.pallas_call(
        kernel,
        out_shape=(
            jax.ShapeDtypeStruct((BS, N * W), F32),
            jax.ShapeDtypeStruct((ROWS, N * W), F32),
        ),
        in_specs=[hbm, hbm, vmem, hbm, vmem, hbm],
        out_specs=(hbm, vmem),
        scratch_shapes=[
            b16(2, 4 * BS, 8 * BS),
            b16(2, 2 * BS, 16 * BS),
            f32(N, 8, BS, W),
            f32(N, 4, BS, W),
            f32(N, 2, 4 * BS, W),
            f32(N, 4 * BS, W),
            f32(N, HB, W), f32(N, HB, W),
            f32(N, BS, W), f32(N, BS, W),
            f32(N, HB, W), f32(N, HB, W),
            f32(N, BS, W), f32(N, BS, W),
            f32(N, 7, ROWS, W),
            f32(4, BS, BS),
            b16(4, BS, 2 * BS), b16(4, BS, 2 * BS),
            b16(8 * BS, 2 * W),
            b16(16 * BS, 2 * W),
            f32(N, BS, W),
            b16(BS, 2 * BS), b16(BS, 2 * BS),
            f32(N, ROWS, W),
            pltpu.SMEM((1, 4, 8), jnp.int32),
            dma(3 * N + 1), dma(N), dma(8, 4), dma(8, 4), dma(N, KINDS), dma(N, KINDS),
        ],
        compiler_params=pltpu.CompilerParams(
            collective_id=0, has_side_effects=True, vmem_limit_bytes=63 * 2**20
        ),
    )(
        jnp.swapaxes(tile_mask, 1, 2),
        leaf_rhs.reshape(4, BS, N * W),
        leaf_inverse,
        parent_rhs[0],
        parent_inverse[0],
        factor[0].reshape(8, BS, 4 * BS),
    )
    solved, leaf = pl.pallas_call(
        hand_on,
        out_shape=(
            jax.ShapeDtypeStruct((BS, N * W), F32),
            jax.ShapeDtypeStruct((ROWS, N * W), F32),
        ),
        in_specs=[vmem, vmem],
        out_specs=(vmem, vmem),
    )(solved, leaf)
    return solved[None], leaf


def solution(mesh):
    placed = (
        P("prow", None),
        P(("prow", "pcol"), None),
        P("pcol", "prow", None),
        P("pcol", "prow", None),
        P("pcol", None, "prow"),
        P("pcol", None, "prow"),
    )
    return jax.shard_map(
        body,
        mesh=mesh,
        in_specs=placed,
        out_specs=(P("pcol", "prow", None), P(("prow", "pcol"), None)),
        check_vma=False,
    )
```
